512 devices in a mesh: grp: 32 (over x_lo, z), seq: 16 (over x_hi, y, core).
Axes of the slice: x: 4 (x_hi: 2, x_lo: 2; x = x_hi * 2 + x_lo), y: 4, z: 16, core: 2. Of those that a mesh axis runs over, the one named last changes fastest.
Arguments:
- cache: bfloat16 [512, 3584, 576], P(('grp', 'seq')), parts along dimension 0, may hold values from -12 to 12
- lengths: int32 [128], P('grp'), parts along dimension 0, may hold values from 896 to 3584, as said below
- owners: int32 [128], P('grp'), parts along dimension 0, may hold values from 0 to 15, as said below
- positions: int32 [128, 12], P('grp'), parts along dimension 0, may hold values from 0 to 11, as said below
- q_nope: bfloat16 [128, 12, 8192], P('grp', None, 'seq'), parts along dimension 0, may hold values from -6 to 6
- q_rope: bfloat16 [128, 12, 4096], P('grp', None, 'seq'), parts along dimension 0, may hold values from -12 to 12
- absorb_weight: bfloat16 [64, 128, 512], P('seq'), may hold values from -0.5 to 0.5
- new_latent: bfloat16 [128, 12, 576], P('grp'), parts along dimension 0, may hold values from -15 to 15
Outputs:
- attn_latent: bfloat16 [128, 12, 32768], P('grp', None, 'seq'), parts along dimension 0
The draws below stay inside these ranges and needn't reach their ends.
There are 32 independent parts, one for each index of `grp`. The reference program is written for one: setup_inputs(seed, part) draws one part's arguments, and reference() takes and returns one part's arrays. A program takes and returns all parts, laid end to end along the dimension named above; an argument that names none is the same for every part. Nothing has to cross between parts.
Inputs may be any that keep to these rules, and one draw needn't show every extreme that they name: `lengths`: one straggler has the full length 3584. The owners of a group are distinct ranks. Step j's tokens have consecutive positions b_j, b_j + 1, b_j + 2 with b_0 = 0 and b_j - b_(j-1) between 1 and 3.
All inputs are finite; a program needn't handle non-finite values.
Results may differ from the reference program's by a relative error of at most 0.015.
Values may be sent and summed in bfloat16 or wider, within the bound.
No kernel may reach another device: no remote copies, remote signals or barrier semaphores. Data moves between devices by JAX's collectives and lax.ppermute only.
A program may use at most 64 MiB of HBM per device.

```python
import math
import jax
import jax.numpy as jnp
from jax import lax

H = 64
KVL = 512
ROPE = 64
NOPE = 128
STEPS = 4
DRAFT = 3
STRAG = 4
CTX = 3584
RANKS = 16
TOKQ = 12


def common_signs(key):
    flips = jax.random.bernoulli(jax.random.fold_in(key, 99), 0.5, (ROPE,))
    return jnp.where(flips, 1.0, -1.0).astype(jnp.float32)


def draw_cache(key, part):
    signs = common_signs(key)
    key = jax.random.fold_in(key, 11)
    key_base, key_small, key_shift, key_place, key_latent = jax.random.split(key, 5)
    base = jax.random.truncated_normal(key_base, -4.0, 4.0, (RANKS, CTX, KVL + ROPE), jnp.float32)
    row_scale = jnp.exp(jax.random.uniform(key_small, (RANKS, CTX, 1), jnp.float32, math.log(0.5), math.log(2.0)))
    shift = 1.5 * jax.random.uniform(key_shift, (KVL + ROPE,), jnp.float32, -1.0, 1.0)
    values = base * row_scale + shift[None, None, :]
    place_keys = jax.random.split(key_place, RANKS)
    planted_rows = jax.vmap(lambda one: jax.random.permutation(one, CTX // 4)[:2])(place_keys)
    latent_part = 0.25 * jax.random.truncated_normal(key_latent, -4.0, 4.0, (RANKS, 2, KVL), jnp.float32) + shift[None, None, :KVL]
    strengths = jnp.asarray([4.0, 3.96875], jnp.float32)
    rope_part = jnp.broadcast_to(strengths[None, :, None] * signs[None, None, :], (RANKS, 2, ROPE))
    planted = jnp.concatenate([latent_part, rope_part], axis=-1)
    rank_index = jnp.arange(RANKS, dtype=jnp.int32)[:, None]
    values = values.at[rank_index, planted_rows].set(planted)
    return values.astype(jnp.bfloat16)


def draw_q_rope(key, part):
    signs = common_signs(key)
    key = jax.random.fold_in(key, 15)
    key_base, key_pick = jax.random.split(key)
    base = jax.random.truncated_normal(key_base, -6.0, 6.0, (STRAG, TOKQ * H, ROPE), jnp.float32)
    pick_keys = jax.random.split(key_pick, STRAG)
    picked = jax.vmap(lambda one: jax.random.permutation(one, TOKQ * H)[:3])(pick_keys)
    strengths = jnp.asarray([12.0, 9.0, 6.0], jnp.float32)
    planted = jnp.broadcast_to(strengths[None, :, None] * signs[None, None, :], (STRAG, 3, ROPE))
    strag_index = jnp.arange(STRAG, dtype=jnp.int32)[:, None]
    values = base.at[strag_index, picked].set(planted)
    return values.reshape(STRAG, TOKQ, H * ROPE).astype(jnp.bfloat16)


def draw_lengths(key, part):
    key = jax.random.fold_in(key, 12)
    key_vals, key_slot = jax.random.split(key)
    values = jax.random.randint(key_vals, (STRAG,), CTX // 4, CTX + 1)
    slot = jax.random.randint(key_slot, (), 0, STRAG)
    return jnp.where(jnp.arange(STRAG) == slot, CTX, values).astype(jnp.int32)


def draw_owners(key, part):
    key = jax.random.fold_in(key, 13)
    combos = RANKS // 2 * STRAG
    start = jax.random.randint(key, (), 0, combos)
    pick = (start + jnp.asarray(part, jnp.int32)) % combos
    stride = 2 * (pick % (RANKS // 2)) + 1
    slot = pick // (RANKS // 2)
    offset = (RANKS - 1 - stride * slot) % RANKS
    index = jnp.arange(STRAG, dtype=jnp.int32)
    return ((stride * index + offset) % RANKS).astype(jnp.int32)


def draw_positions(key, part):
    key = jax.random.fold_in(key, 14)
    accepted = jax.random.randint(key, (STRAG, STEPS), 1, 4)
    accepted = accepted.at[0].set(3)
    starts = jnp.cumsum(accepted, axis=1) - accepted
    offsets = jnp.arange(DRAFT, dtype=jnp.int32)
    return (starts[:, :, None] + offsets[None, None, :]).reshape(STRAG, STEPS * DRAFT).astype(jnp.int32)


def block_levels(rng, extent, cuts, smallest, largest):
    factor_of = 1.0
    for position, parts in cuts:
        draws = jax.random.uniform(jax.random.fold_in(jax.random.fold_in(rng, 6), position), (parts,), jnp.float32, smallest / len(cuts), largest / len(cuts))
        factor_of = factor_of * jnp.repeat(jnp.exp(draws), extent[position] // parts).reshape((-1,) + (1,) * (len(extent) - 1 - position))
    return factor_of


def noise(stream_key, dims, deviation, limit, cuts=(), held_as=jnp.bfloat16):
    drawn = jax.random.normal(stream_key, dims, jnp.float32) * deviation
    if len(cuts) > 0:
        drawn = block_levels(stream_key, dims, cuts, -0.22, 0.18) * drawn
    return jnp.clip(drawn, min=-limit, max=limit).astype(held_as)


def setup_inputs(seed: int = 0, part: int = 0) -> dict:
    keys = jax.random.split(jax.random.key(seed), 9)
    part_splits = jax.random.split(jax.random.fold_in(keys[8], part), 9)
    cache = draw_cache(jax.random.fold_in(jax.random.fold_in(keys[8], part), 71), part)
    lengths = draw_lengths(jax.random.fold_in(jax.random.fold_in(keys[8], part), 71), part)
    owners = draw_owners(jax.random.fold_in(jax.random.fold_in(keys[8], part), 71), part)
    positions = draw_positions(jax.random.fold_in(jax.random.fold_in(keys[8], part), 71), part)
    q_nope = noise(part_splits[4], (STRAG, TOKQ, H * NOPE), 1.0, 6.0, ((2, 16),))
    q_rope = draw_q_rope(jax.random.fold_in(jax.random.fold_in(keys[8], part), 71), part)
    absorb_weight = noise(keys[6], (H, NOPE, KVL), NOPE ** -0.5, 0.5, ((0, 16),))
    new_latent = noise(part_splits[7], (STRAG, TOKQ, KVL + ROPE), 2.5, 15.0)
    return dict(cache=cache, lengths=lengths, owners=owners, positions=positions, q_nope=q_nope, q_rope=q_rope, absorb_weight=absorb_weight, new_latent=new_latent)


def reference(cache, lengths, owners, positions, q_nope, q_rope, absorb_weight, new_latent):
    score_scale = 1.0 / math.sqrt(NOPE + ROPE)
    piece_rows = CTX // RANKS
    query_nope = q_nope.reshape(STRAG, TOKQ, H, NOPE).astype(jnp.float32)
    absorbed = jnp.einsum('sthn,hnc->sthc', query_nope, absorb_weight.astype(jnp.float32)).astype(jnp.bfloat16)
    query_rope = q_rope.reshape(STRAG, TOKQ, H, ROPE)
    query = jnp.concatenate([absorbed, query_rope], axis=-1).reshape(STRAG, TOKQ * H, KVL + ROPE)
    results = []
    for index in range(STRAG):
        owner_keys = lax.dynamic_index_in_dim(cache, owners[index], 0, keepdims=False)
        pieces = owner_keys.reshape(RANKS, piece_rows, KVL + ROPE).astype(jnp.float32)
        rows_query = query[index].astype(jnp.float32)
        scores = jnp.einsum('qc,prc->pqr', rows_query, pieces) * score_scale
        slot_index = jnp.arange(CTX, dtype=jnp.int32).reshape(RANKS, 1, piece_rows)
        visible = slot_index < lengths[index]
        scores = jnp.where(visible, scores, -jnp.inf)
        token_pos = positions[index]
        new_keys = new_latent[index].astype(jnp.float32)
        new_scores = jnp.dot(rows_query, new_keys.T) * score_scale
        query_pos = jnp.repeat(token_pos, H)
        new_seen = token_pos[None, :] <= query_pos[:, None]
        new_scores = jnp.where(new_seen, new_scores, -jnp.inf)
        row_top = jnp.maximum(lax.optimization_barrier(jnp.max(scores, axis=(0, 2))), lax.optimization_barrier(jnp.max(new_scores, axis=1)))
        weights = jnp.where(visible, jnp.exp(scores - row_top[None, :, None]), 0.0)
        new_weights = jnp.where(new_seen, jnp.exp(new_scores - row_top[:, None]), 0.0)
        total = lax.optimization_barrier(jnp.sum(weights, axis=(0, 2))) + lax.optimization_barrier(jnp.sum(new_weights, axis=1))
        partial_value = jnp.einsum('pqr,prc->pqc', weights.astype(jnp.bfloat16).astype(jnp.float32), pieces[:, :, :KVL])
        new_part = jnp.dot(new_weights.astype(jnp.bfloat16).astype(jnp.float32), new_keys[:, :KVL])
        partial_value = partial_value.at[0].add(new_part)
        partial_value = lax.optimization_barrier(partial_value.astype(jnp.bfloat16)).astype(jnp.float32)
        summed = lax.optimization_barrier(jnp.sum(partial_value, axis=0))
        results.append((summed / total[:, None]).astype(jnp.bfloat16).reshape(TOKQ, H * KVL))
    return jnp.stack(results)
```

```python
import functools
import math

import jax
import jax.numpy as jnp
from jax import lax
from jax.experimental import pallas as pl
from jax.experimental.pallas import tpu as pltpu
from jax.sharding import PartitionSpec as P

KVL = 512
ROPE = 64
NOPE = 128
NEW_PAD = 128
CHUNK = 512
HEAD = NEW_PAD + CHUNK
F32 = jnp.float32
BF16 = jnp.bfloat16
HIDDEN = -1e30
WIDE = 640
VMEM = pltpu.VMEM


def iota2(shape, dim):
    return lax.broadcasted_iota(jnp.int32, shape, dim)


def absorb_kernel(strags, toks, heads, owners_ref, nope_hbm, rope_hbm, weight_hbm, out_hbm, nope_ref, rope_ref, weight_ref, nope_rows, rope_rows, slots, sems, out_sems):
    copies = [
        pltpu.make_async_copy(src, dst, sems.at[i])
        for i, (src, dst) in enumerate(((nope_hbm, nope_ref), (rope_hbm, rope_ref), (weight_hbm, weight_ref)))
    ]
    for copy in copies:
        copy.start()
    rows = strags * toks * heads
    per = toks * heads
    wide = (rows, toks * strags)
    row, col = iota2(wide, 0), iota2(wide, 1)
    pick = (col == (row % per) // heads * strags + row // per).astype(F32).astype(BF16)
    fold = (iota2((heads * ROPE, ROPE), 0) % ROPE == iota2((heads * ROPE, ROPE), 1)).astype(F32).astype(BF16)
    tail = (rows, WIDE - KVL - ROPE)
    marks = (iota2(tail, 1) == iota2(tail, 0) % per // heads).astype(F32).astype(BF16)

    def spread(ref, width):
        copied = jnp.dot(pick, ref[...].astype(BF16), preferred_element_type=F32)
        shape = (rows, heads * width)
        own = iota2(shape, 1) // width == iota2(shape, 0) % heads
        return jnp.where(own, copied, 0.0).astype(BF16)

    copies[0].wait()
    copies[1].wait()
    for t in range(toks):
        nope_rows[t * strags : (t + 1) * strags, :] = nope_ref[t].astype(F32)
        rope_rows[t * strags : (t + 1) * strags, :] = rope_ref[t].astype(F32)
    roped = jnp.dot(spread(rope_rows, ROPE), fold, preferred_element_type=F32).astype(BF16)
    slots[:, KVL:] = jnp.concatenate([roped, marks], axis=1)
    expanded = spread(nope_rows, NOPE)
    copies[2].wait()
    slots[:, :KVL] = jnp.dot(expanded, weight_ref[...], preferred_element_type=F32).astype(BF16)
    leaving = [
        pltpu.make_async_copy(slots.at[pl.ds(s * per, per)], out_hbm.at[owners_ref[s]], out_sems.at[s]) for s in range(strags)
    ]
    for copy in leaving:
        copy.start()
    for copy in leaving:
        copy.wait()


def straggler_here(strags, me_ref, owners_ref):
    mine = jnp.int32(-1)
    for s in range(strags):
        mine = jnp.where(owners_ref[s] == me_ref[0], s, mine)
    return mine


def stage_kernel(strags, me_ref, owners_ref, lengths_ref, new_ref, keys_ref, out_ref, tail, sems):
    mine = straggler_here(strags, me_ref, owners_ref)
    width = keys_ref.shape[0]
    count = out_ref.shape[1] - NEW_PAD

    @pl.when(mine >= 0)
    def _():
        copies = [
            pltpu.make_async_copy(
                keys_ref.at[:, pl.ds(0, count)], out_ref.at[pl.ds(0, width), pl.ds(NEW_PAD, count)], sems.at[0]
            ),
            pltpu.make_async_copy(new_ref.at[mine], out_ref.at[:, pl.ds(0, NEW_PAD)], sems.at[1]),
            pltpu.make_async_copy(tail, out_ref.at[pl.ds(width, WIDE - width), pl.ds(NEW_PAD, count)], sems.at[2]),
        ]
        copies[0].start()
        copies[1].start()
        tail[...] = jnp.where(iota2(tail.shape, 1) < lengths_ref[mine], 0.0, HIDDEN).astype(BF16)
        copies[2].start()
        for copy in copies:
            copy.wait()


def attend_kernel(strags, me_ref, owners_ref, lengths_ref, query_ref, head_ref, keys_ref, out_ref, keys, raw_even, raw_odd, acc, total, top_even, top_odd, answer, key_sems, sem):
    mine = straggler_here(strags, me_ref, owners_ref)
    width, ctx = keys_ref.shape
    count = ctx // CHUNK
    factor = math.log2(math.e) / math.sqrt(NOPE + ROPE)

    def key_copy(i):
        part = pl.ds(pl.multiple_of(i * CHUNK, CHUNK), CHUNK)
        return pltpu.make_async_copy(keys_ref.at[:, part], keys.at[pl.ds(0, width), part], key_sems.at[i])

    def score(keys_part, raw, size, top_before, top_after):
        part = jnp.dot(query_ref[...], keys_part, preferred_element_type=F32)
        raw[:, :size] = part
        peak = part[:, :128]
        for j in range(128, size, 128):
            peak = jnp.maximum(peak, part[:, j : j + 128])
        peak = jnp.broadcast_to(jnp.max(peak, axis=1, keepdims=True), peak.shape)
        top_after[...] = peak if top_before is None else jnp.maximum(top_before[...], peak)

    def weigh(values_part, raw, size, top_before, top_after):
        top = top_after[...]
        shift = top * factor
        pieces = [jnp.exp2(raw[:, j : j + 128] * factor - shift) for j in range(0, size, 128)]
        mass = pieces[0]
        for piece in pieces[1:]:
            mass = mass + piece
        weight = pieces[0] if size == 128 else jnp.concatenate(pieces, axis=1)
        value = lax.dot_general(weight.astype(BF16), values_part, (((1,), (1,)), ((), ())), preferred_element_type=F32)
        if top_before is None:
            total[...] = mass
            acc[...] = value
            return
        fade = jnp.exp2(top_before * factor - shift)
        total[...] = total[...] * fade + mass
        for j in range(0, KVL, 128):
            acc[:, j : j + 128] = acc[:, j : j + 128] * fade + value[:, j : j + 128]

    @pl.when(mine >= 0)
    def _():
        for i in range(count):
            key_copy(i).start()
        keys[width:, :] = jnp.where(iota2((WIDE - width, ctx), 1) < lengths_ref[mine], 0.0, HIDDEN).astype(BF16)

        def cached(i, depth):
            return keys[:depth, pl.ds(pl.multiple_of(i * CHUNK, CHUNK), CHUNK)]

        score(head_ref[:, :NEW_PAD], raw_odd, NEW_PAD, None, top_odd)
        score(head_ref[:, NEW_PAD:], raw_even, CHUNK, top_odd, top_even)
        weigh(head_ref[:KVL, :NEW_PAD], raw_odd, NEW_PAD, None, top_odd)
        key_copy(0).wait()

        @pl.loop(0, count // 2)
        def _(pair):
            i = pair * 2
            key_copy(i + 1).wait()
            key_copy(i + 2).wait()
            before = top_odd[...]
            score(cached(i + 1, WIDE), raw_odd, CHUNK, top_even, top_odd)
            weigh(cached(i, KVL), raw_even, CHUNK, before, top_even)
            before = top_even[...]
            score(cached(i + 2, WIDE), raw_even, CHUNK, top_odd, top_even)
            weigh(cached(i + 1, KVL), raw_odd, CHUNK, before, top_odd)

        weigh(keys[:KVL, ctx - CHUNK :], raw_even, CHUNK, top_odd[...], top_even)
        inverse = 1.0 / jnp.sum(total[...], axis=1, keepdims=True)
        answer[...] = (acc[...] * inverse).astype(BF16)
        copy = pltpu.make_async_copy(answer, out_ref, sem)
        copy.start()
        copy.wait()


def collect_kernel(strags, toks, heads, owners_ref, got_ref, out_ref, held):
    per = toks * heads
    for s in range(strags):
        held[s * per : (s + 1) * per, :] = got_ref[owners_ref[s]]
    shape = (toks * strags, strags * per)
    row, col = iota2(shape, 0), iota2(shape, 1)
    for h in range(heads):
        pick = (col == row % strags * per + row // strags * heads + h).astype(F32).astype(BF16)
        lined = jnp.dot(pick, held[...], preferred_element_type=F32).astype(BF16)
        for t in range(toks):
            out_ref[t, :, h * KVL : (h + 1) * KVL] = lined[t * strags : (t + 1) * strags]


def shards(cache, lengths, owners, positions, q_nope, q_rope, absorb_weight, new_latent):
    ranks = lax.axis_size("seq")
    me = lax.axis_index("seq").astype(jnp.int32).reshape(1)
    strags, toks = positions.shape
    heads = absorb_weight.shape[0]
    per = toks * heads
    ctx, width = cache.shape[1:]
    rows = ranks * per
    smem = pl.BlockSpec(memory_space=pltpu.SMEM)
    vmem = pl.BlockSpec(memory_space=pltpu.VMEM)
    anyspace = pl.BlockSpec(memory_space=pl.ANY)
    sending = pl.pallas_call(
        functools.partial(absorb_kernel, strags, toks, heads),
        out_shape=jax.ShapeDtypeStruct((ranks, per, WIDE), BF16),
        in_specs=[smem, anyspace, anyspace, anyspace],
        out_specs=anyspace,
        scratch_shapes=[
            VMEM((toks, strags, heads * NOPE), BF16),
            VMEM((toks, strags, heads * ROPE), BF16),
            VMEM((heads * NOPE, KVL), BF16),
            VMEM((toks * strags, heads * NOPE), F32),
            VMEM((toks * strags, heads * ROPE), F32),
            VMEM((strags * per, WIDE), BF16),
            pltpu.SemaphoreType.DMA((3,)),
            pltpu.SemaphoreType.DMA((strags,)),
        ],
        compiler_params=pltpu.CompilerParams(vmem_limit_bytes=60 * 2**20),
        name="absorb",
    )(
        owners,
        jnp.transpose(q_nope, (1, 0, 2)),
        jnp.transpose(q_rope, (1, 0, 2)),
        absorb_weight.reshape(heads * NOPE, KVL),
    )
    query = lax.all_to_all(sending, "seq", split_axis=0, concat_axis=0, tiled=True).reshape(rows, WIDE)
    seen = positions[:, None, :] <= positions[:, :, None]
    hidden = jnp.where(seen, 0.0, HIDDEN).astype(BF16)
    fresh = jnp.concatenate([jnp.transpose(new_latent, (0, 2, 1)), hidden], axis=1)
    fresh = jnp.pad(fresh, ((0, 0), (0, WIDE - width - toks), (0, 0)))
    unused = jnp.where(jnp.arange(WIDE) < width, 0.0, HIDDEN).astype(BF16)
    unused = jnp.broadcast_to(unused[None, :, None], (strags, WIDE, NEW_PAD - toks))
    fresh = jnp.concatenate([fresh, unused], axis=2)
    keys = jnp.transpose(cache[0])
    staged = pl.pallas_call(
        functools.partial(stage_kernel, strags),
        out_shape=jax.ShapeDtypeStruct((WIDE, HEAD), BF16),
        in_specs=[smem, smem, smem, anyspace, anyspace],
        out_specs=anyspace,
        scratch_shapes=[VMEM((WIDE - width, HEAD - NEW_PAD), BF16), pltpu.SemaphoreType.DMA((3,))],
        compiler_params=pltpu.CompilerParams(vmem_limit_bytes=24 * 2**20),
        cost_estimate=pl.CostEstimate(flops=0, bytes_accessed=4 * WIDE * HEAD, transcendentals=0),
        name="stage",
    )(me, owners, lengths, fresh, keys)
    answer = pl.pallas_call(
        functools.partial(attend_kernel, strags),
        out_shape=jax.ShapeDtypeStruct((rows, KVL), BF16),
        in_specs=[smem, smem, smem, vmem, vmem, anyspace],
        out_specs=anyspace,
        scratch_shapes=[
            VMEM((WIDE, ctx), BF16),
            VMEM((rows, CHUNK), F32),
            VMEM((rows, CHUNK), F32),
            VMEM((rows, KVL), F32),
            VMEM((rows, 128), F32),
            VMEM((rows, 128), F32),
            VMEM((rows, 128), F32),
            VMEM((rows, KVL), BF16),
            pltpu.SemaphoreType.DMA((ctx // CHUNK,)),
            pltpu.SemaphoreType.DMA,
        ],
        compiler_params=pltpu.CompilerParams(vmem_limit_bytes=48 * 2**20),
        name="attend",
    )(me, owners, lengths, query, staged, keys)
    got = lax.all_to_all(answer.reshape(ranks, per, KVL), "seq", split_axis=0, concat_axis=0, tiled=True)
    out = pl.pallas_call(
        functools.partial(collect_kernel, strags, toks, heads),
        out_shape=jax.ShapeDtypeStruct((toks, strags, heads * KVL), BF16),
        in_specs=[smem, vmem],
        out_specs=vmem,
        scratch_shapes=[VMEM((strags * per, KVL), BF16)],
        compiler_params=pltpu.CompilerParams(vmem_limit_bytes=32 * 2**20),
        name="collect",
    )(owners, got)
    return jnp.transpose(out, (1, 0, 2))


def solution(mesh):
    in_specs = (
        P(("grp", "seq"), None, None),
        P("grp"),
        P("grp"),
        P("grp", None),
        P("grp", None, "seq"),
        P("grp", None, "seq"),
        P("seq", None, None),
        P("grp", None, None),
    )
    out_specs = P("grp", None, "seq")
    return jax.shard_map(shards, mesh=mesh, in_specs=in_specs, out_specs=out_specs, check_vma=False)
```

```python
import functools
import math

import jax
import jax.numpy as jnp
from jax import lax
from jax.experimental import pallas as pl
from jax.experimental.pallas import tpu as pltpu
from jax.sharding import PartitionSpec as P

KVL = 512
ROPE = 64
NOPE = 128
NEW_PAD = 128
CHUNK = 512
HEAD = NEW_PAD + CHUNK // 2
F32 = jnp.float32
BF16 = jnp.bfloat16
HIDDEN = -1e30
WIDE = 640
VMEM = pltpu.VMEM


def iota2(shape, dim):
    return lax.broadcasted_iota(jnp.int32, shape, dim)


def absorb_kernel(strags, toks, heads, owners_ref, nope_hbm, rope_hbm, weight_hbm, out_hbm, nope_ref, rope_ref, weight_ref, nope_rows, rope_rows, slots, sems, out_sems):
    copies = [
        pltpu.make_async_copy(src, dst, sems.at[i])
        for i, (src, dst) in enumerate(((nope_hbm, nope_ref), (rope_hbm, rope_ref), (weight_hbm, weight_ref)))
    ]
    for copy in copies:
        copy.start()
    per = toks * heads
    rows = strags * per

    def parts_of(shape):
        row = iota2(shape, 0)
        strag = sum((row >= s * per).astype(jnp.int32) for s in range(1, strags))
        line = row - strag * per
        return strag, line // heads, line & (heads - 1)

    shape = (rows, toks * strags)
    strag, tok, _ = parts_of(shape)
    pick = (iota2(shape, 1) == tok * strags + strag).astype(F32).astype(BF16)
    shape = (heads * ROPE, ROPE)
    fold = ((iota2(shape, 0) & (ROPE - 1)) == iota2(shape, 1)).astype(F32).astype(BF16)
    shape = (rows, WIDE - KVL - ROPE)
    marks = (iota2(shape, 1) == parts_of(shape)[1]).astype(F32).astype(BF16)
    _, _, head = parts_of((rows, 1))

    def spread(ref, width):
        copied = jnp.dot(pick, ref[...].astype(BF16), preferred_element_type=F32)
        pieces = []
        for h in range(heads):
            pieces.append(jnp.where(head == h, copied[:, h * width : (h + 1) * width], 0.0))
        return pieces

    copies[0].wait()
    copies[1].wait()
    for t in range(toks):
        nope_rows[t * strags : (t + 1) * strags, :] = nope_ref[t].astype(F32)
        rope_rows[t * strags : (t + 1) * strags, :] = rope_ref[t].astype(F32)
    expanded = jnp.concatenate(spread(nope_rows, NOPE), axis=1).astype(BF16)
    roped = sum(spread(rope_rows, ROPE)).astype(BF16)
    slots[:, KVL:] = jnp.concatenate([roped, marks], axis=1)
    copies[2].wait()
    slots[:, :KVL] = jnp.dot(expanded, weight_ref[...], preferred_element_type=F32).astype(BF16)
    leaving = [
        pltpu.make_async_copy(slots.at[pl.ds(s * per, per)], out_hbm.at[owners_ref[s]], out_sems.at[s]) for s in range(strags)
    ]
    for copy in leaving:
        copy.start()
    for copy in leaving:
        copy.wait()


def straggler_here(strags, info_ref):
    mine = jnp.int32(-1)
    for s in range(strags):
        mine = jnp.where(info_ref[1 + s] == info_ref[0], s, mine)
    return mine


def stage_kernel(strags, info_ref, new_ref, keys_ref, out_ref, tail_ref, hidden, sems):
    mine = straggler_here(strags, info_ref)
    width = keys_ref.shape[0]
    spare = WIDE - width
    count = out_ref.shape[1] - NEW_PAD

    @pl.when(mine >= 0)
    def _():
        copies = [
            pltpu.make_async_copy(
                keys_ref.at[:, pl.ds(0, count)], out_ref.at[pl.ds(0, width), pl.ds(NEW_PAD, count)], sems.at[0]
            ),
            pltpu.make_async_copy(new_ref.at[mine], out_ref.at[:, pl.ds(0, NEW_PAD)], sems.at[1]),
            pltpu.make_async_copy(
                hidden.at[:, pl.ds(0, count)], out_ref.at[pl.ds(width, spare), pl.ds(NEW_PAD, count)], sems.at[2]
            ),
            pltpu.make_async_copy(hidden.at[:, pl.ds(count, tail_ref.shape[1])], tail_ref, sems.at[3]),
        ]
        copies[0].start()
        copies[1].start()
        length = info_ref[1 + strags + mine]
        hidden[...] = jnp.where(iota2(hidden.shape, 1) < length, 0.0, HIDDEN).astype(BF16)
        copies[2].start()
        copies[3].start()
        for copy in copies:
            copy.wait()


def attend_kernel(strags, info_ref, query_ref, head_ref, tail_ref, keys_ref, out_ref, keys, raw_even, raw_odd, acc, total, top_even, top_odd, key_sems, tail_sem):
    mine = straggler_here(strags, info_ref)
    width, ctx = keys_ref.shape
    first = head_ref.shape[1] - NEW_PAD
    count = (ctx - first) // CHUNK
    last = ctx - first - count * CHUNK
    factor = math.log2(math.e) / math.sqrt(NOPE + ROPE)

    def key_copy(i, size=CHUNK):
        return pltpu.make_async_copy(
            keys_ref.at[:, pl.ds(pl.multiple_of(first + i * CHUNK, 128), size)],
            keys.at[pl.ds(0, width), pl.ds(pl.multiple_of(i * CHUNK, 128), size)],
            key_sems.at[i],
        )

    def score(keys_part, raw, size, top_before, top_after):
        part = jnp.dot(query_ref[...], keys_part, preferred_element_type=F32)
        raw[:, :size] = part
        peak = part[:, :128]
        for j in range(128, size, 128):
            peak = jnp.maximum(peak, part[:, j : j + 128])
        peak = jnp.broadcast_to(jnp.max(peak, axis=1, keepdims=True), peak.shape)
        top_after[...] = peak if top_before is None else jnp.maximum(top_before[...], peak)

    def weigh(values_part, raw, size, top_before, top_after):
        top = top_after[...]
        shift = top * factor
        pieces = [jnp.exp2(raw[:, j : j + 128] * factor - shift) for j in range(0, size, 128)]
        mass = pieces[0]
        for piece in pieces[1:]:
            mass = mass + piece
        weight = pieces[0] if size == 128 else jnp.concatenate(pieces, axis=1)
        value = lax.dot_general(weight.astype(BF16), values_part, (((1,), (1,)), ((), ())), preferred_element_type=F32)
        if top_before is None:
            total[...] = mass
            acc[...] = value
            return
        fade = jnp.exp2(top_before * factor - shift)
        total[...] = total[...] * fade + mass
        for j in range(0, KVL, 128):
            acc[:, j : j + 128] = acc[:, j : j + 128] * fade + value[:, j : j + 128]

    @pl.when(mine >= 0)
    def _():
        masks = pltpu.make_async_copy(tail_ref, keys.at[pl.ds(width, WIDE - width)], tail_sem)
        masks.start()
        for i in range(count):
            key_copy(i).start()
        key_copy(count, last).start()

        def cached(i, depth, size=CHUNK):
            return keys[:depth, pl.ds(pl.multiple_of(i * CHUNK, 128), size)]

        score(head_ref[:, :NEW_PAD], raw_odd, NEW_PAD, None, top_odd)
        score(head_ref[:, NEW_PAD:], raw_even, first, top_odd, top_even)
        weigh(head_ref[:KVL, :NEW_PAD], raw_odd, NEW_PAD, None, top_odd)
        masks.wait()
        key_copy(0).wait()
        before = top_odd[...]
        score(cached(0, WIDE), raw_odd, CHUNK, top_even, top_odd)
        weigh(head_ref[:KVL, NEW_PAD:], raw_even, first, before, top_even)

        @pl.loop(0, count // 2 - 1)
        def _(pair):
            i = pair * 2
            key_copy(i + 1).wait()
            key_copy(i + 2).wait()
            before = top_even[...]
            score(cached(i + 1, WIDE), raw_even, CHUNK, top_odd, top_even)
            weigh(cached(i, KVL), raw_odd, CHUNK, before, top_odd)
            before = top_odd[...]
            score(cached(i + 2, WIDE), raw_odd, CHUNK, top_even, top_odd)
            weigh(cached(i + 1, KVL), raw_even, CHUNK, before, top_even)

        key_copy(count - 1).wait()
        key_copy(count, last).wait()
        before = top_even[...]
        score(cached(count - 1, WIDE), raw_even, CHUNK, top_odd, top_even)
        weigh(cached(count - 2, KVL), raw_odd, CHUNK, before, top_odd)
        before = top_odd[...]
        score(cached(count, WIDE, last), raw_odd, last, top_even, top_odd)
        weigh(cached(count - 1, KVL), raw_even, CHUNK, before, top_even)
        weigh(cached(count, KVL, last), raw_odd, last, top_even[...], top_odd)
        inverse = 1.0 / jnp.sum(total[...], axis=1, keepdims=True)
        out_ref[...] = (acc[...] * inverse).astype(BF16)


def collect_kernel(strags, toks, heads, starts_ref, got_ref, out_ref, held):
    per = toks * heads
    for s in range(strags):
        held[s * per : (s + 1) * per, :] = got_ref[pl.ds(pl.multiple_of(starts_ref[s], 16), per), :]
    shape = (toks * strags, strags * per)
    row, col = iota2(shape, 0), iota2(shape, 1)
    for h in range(heads):
        pick = (col == row % strags * per + row // strags * heads + h).astype(F32).astype(BF16)
        lined = jnp.dot(pick, held[...], preferred_element_type=F32).astype(BF16)
        for t in range(toks):
            out_ref[t, :, h * KVL : (h + 1) * KVL] = lined[t * strags : (t + 1) * strags]


def shards(cache, lengths, owners, positions, q_nope, q_rope, absorb_weight, new_latent):
    ranks = lax.axis_size("seq")
    me = lax.axis_index("seq").astype(jnp.int32).reshape(1)
    strags, toks = positions.shape
    heads = absorb_weight.shape[0]
    per = toks * heads
    ctx, width = cache.shape[1:]
    rows = ranks * per
    smem = pl.BlockSpec(memory_space=pltpu.SMEM)
    vmem = pl.BlockSpec(memory_space=pltpu.VMEM)
    anyspace = pl.BlockSpec(memory_space=pl.ANY)
    sending = pl.pallas_call(
        functools.partial(absorb_kernel, strags, toks, heads),
        out_shape=jax.ShapeDtypeStruct((ranks, per, WIDE), BF16),
        in_specs=[smem, anyspace, anyspace, anyspace],
        out_specs=anyspace,
        scratch_shapes=[
            VMEM((toks, strags, heads * NOPE), BF16),
            VMEM((toks, strags, heads * ROPE), BF16),
            VMEM((heads * NOPE, KVL), BF16),
            VMEM((toks * strags, heads * NOPE), F32),
            VMEM((toks * strags, heads * ROPE), F32),
            VMEM((strags * per, WIDE), BF16),
            pltpu.SemaphoreType.DMA((3,)),
            pltpu.SemaphoreType.DMA((strags,)),
        ],
        compiler_params=pltpu.CompilerParams(vmem_limit_bytes=60 * 2**20),
        name="absorb",
    )(
        owners,
        jnp.transpose(q_nope, (1, 0, 2)),
        jnp.transpose(q_rope, (1, 0, 2)),
        absorb_weight.reshape(heads * NOPE, KVL),
    )
    query = lax.all_to_all(sending, "seq", split_axis=0, concat_axis=0, tiled=True).reshape(rows, WIDE)
    seen = positions[:, None, :] <= positions[:, :, None]
    hidden = jnp.where(seen, 0.0, HIDDEN).astype(BF16)
    fresh = jnp.concatenate([jnp.transpose(new_latent, (0, 2, 1)), hidden], axis=1)
    fresh = jnp.pad(fresh, ((0, 0), (0, WIDE - width - toks), (0, 0)))
    unused = jnp.where(jnp.arange(WIDE) < width, 0.0, HIDDEN).astype(BF16)
    unused = jnp.broadcast_to(unused[None, :, None], (strags, WIDE, NEW_PAD - toks))
    fresh = jnp.concatenate([fresh, unused], axis=2)
    keys = jnp.transpose(cache[0])
    info = jnp.concatenate([me, owners, lengths])
    late = ctx - (HEAD - NEW_PAD)
    staged, masks = pl.pallas_call(
        functools.partial(stage_kernel, strags),
        out_shape=[jax.ShapeDtypeStruct((WIDE, HEAD), BF16), jax.ShapeDtypeStruct((WIDE - width, late), BF16)],
        in_specs=[smem, anyspace, anyspace],
        out_specs=[anyspace, anyspace],
        scratch_shapes=[VMEM((WIDE - width, ctx), BF16), pltpu.SemaphoreType.DMA((4,))],
        compiler_params=pltpu.CompilerParams(vmem_limit_bytes=24 * 2**20),
        cost_estimate=pl.CostEstimate(flops=0, bytes_accessed=4 * WIDE * HEAD, transcendentals=0),
        name="stage",
    )(info, fresh, keys)
    answer = pl.pallas_call(
        functools.partial(attend_kernel, strags),
        out_shape=jax.ShapeDtypeStruct((rows, KVL), BF16),
        in_specs=[smem, vmem, vmem, anyspace, anyspace],
        out_specs=vmem,
        scratch_shapes=[
            VMEM((WIDE, late), BF16),
            VMEM((rows, CHUNK), F32),
            VMEM((rows, CHUNK), F32),
            VMEM((rows, KVL), F32),
            VMEM((rows, 128), F32),
            VMEM((rows, 128), F32),
            VMEM((rows, 128), F32),
            pltpu.SemaphoreType.DMA((late // CHUNK + 1,)),
            pltpu.SemaphoreType.DMA,
        ],
        compiler_params=pltpu.CompilerParams(vmem_limit_bytes=48 * 2**20),
        name="attend",
    )(info, query, staged, masks, keys)
    got = lax.all_to_all(answer.reshape(ranks, per, KVL), "seq", split_axis=0, concat_axis=0, tiled=True)
    out = pl.pallas_call(
        functools.partial(collect_kernel, strags, toks, heads),
        out_shape=jax.ShapeDtypeStruct((toks, strags, heads * KVL), BF16),
        in_specs=[smem, vmem],
        out_specs=vmem,
        scratch_shapes=[VMEM((strags * per, KVL), BF16)],
        compiler_params=pltpu.CompilerParams(vmem_limit_bytes=32 * 2**20),
        name="collect",
    )(owners * per, got.reshape(rows, KVL))
    return jnp.transpose(out, (1, 0, 2))


def solution(mesh):
    in_specs = (
        P(("grp", "seq"), None, None),
        P("grp"),
        P("grp"),
        P("grp", None),
        P("grp", None, "seq"),
        P("grp", None, "seq"),
        P("seq", None, None),
        P("grp", None, None),
    )
    out_specs = P("grp", None, "seq")
    return jax.shard_map(shards, mesh=mesh, in_specs=in_specs, out_specs=out_specs, check_vma=False)
```

```python
import functools
import math

import jax
import jax.numpy as jnp
from jax import lax
from jax.experimental import pallas as pl
from jax.experimental.pallas import tpu as pltpu
from jax.sharding import PartitionSpec as P

KVL = 512
ROPE = 64
NOPE = 128
NEW_PAD = 128
CHUNK = 512
HEAD = NEW_PAD + CHUNK
F32 = jnp.float32
BF16 = jnp.bfloat16
HIDDEN = -1e30
WIDE = 640
VMEM = pltpu.VMEM


def iota2(shape, dim):
    return lax.broadcasted_iota(jnp.int32, shape, dim)


def absorb_kernel(strags, toks, heads, owners_ref, nope_hbm, rope_hbm, weight_hbm, out_hbm, nope_ref, rope_ref, weight_ref, nope_rows, rope_rows, slots, sems, out_sems):
    copies = [
        pltpu.make_async_copy(src, dst, sems.at[i])
        for i, (src, dst) in enumerate(((nope_hbm, nope_ref), (rope_hbm, rope_ref), (weight_hbm, weight_ref)))
    ]
    for copy in copies:
        copy.start()
    per = toks * heads
    rows = strags * per

    def parts_of(shape):
        row = iota2(shape, 0)
        strag = sum((row >= s * per).astype(jnp.int32) for s in range(1, strags))
        line = row - strag * per
        return strag, line // heads, line & (heads - 1)

    shape = (rows, toks * strags)
    strag, tok, _ = parts_of(shape)
    pick = (iota2(shape, 1) == tok * strags + strag).astype(F32).astype(BF16)
    shape = (heads * ROPE, ROPE)
    fold = ((iota2(shape, 0) & (ROPE - 1)) == iota2(shape, 1)).astype(F32).astype(BF16)
    shape = (rows, WIDE - KVL - ROPE)
    marks = (iota2(shape, 1) == parts_of(shape)[1]).astype(F32).astype(BF16)
    _, _, head = parts_of((rows, 1))

    def spread(ref, width):
        copied = jnp.dot(pick, ref[...].astype(BF16), preferred_element_type=F32)
        pieces = []
        for h in range(heads):
            pieces.append(jnp.where(head == h, copied[:, h * width : (h + 1) * width], 0.0))
        return pieces

    copies[0].wait()
    copies[1].wait()
    for t in range(toks):
        nope_rows[t * strags : (t + 1) * strags, :] = nope_ref[t].astype(F32)
        rope_rows[t * strags : (t + 1) * strags, :] = rope_ref[t].astype(F32)
    expanded = jnp.concatenate(spread(nope_rows, NOPE), axis=1).astype(BF16)
    roped = sum(spread(rope_rows, ROPE)).astype(BF16)
    slots[:, KVL:] = jnp.concatenate([roped, marks], axis=1)
    copies[2].wait()
    slots[:, :KVL] = jnp.dot(expanded, weight_ref[...], preferred_element_type=F32).astype(BF16)
    leaving = [
        pltpu.make_async_copy(slots.at[pl.ds(s * per, per)], out_hbm.at[owners_ref[s]], out_sems.at[s]) for s in range(strags)
    ]
    for copy in leaving:
        copy.start()
    for copy in leaving:
        copy.wait()


def straggler_here(strags, info_ref):
    mine = jnp.int32(-1)
    for s in range(strags):
        mine = jnp.where(info_ref[1 + s] == info_ref[0], s, mine)
    return mine


def stage_kernel(strags, info_ref, new_ref, keys_ref, out_ref, tail_ref, hidden, sems):
    mine = straggler_here(strags, info_ref)
    width = keys_ref.shape[0]
    spare = WIDE - width
    count = out_ref.shape[1] - NEW_PAD

    @pl.when(mine >= 0)
    def _():
        copies = [
            pltpu.make_async_copy(
                keys_ref.at[:, pl.ds(0, count)], out_ref.at[pl.ds(0, width), pl.ds(NEW_PAD, count)], sems.at[0]
            ),
            pltpu.make_async_copy(new_ref.at[mine], out_ref.at[:, pl.ds(0, NEW_PAD)], sems.at[1]),
            pltpu.make_async_copy(
                hidden.at[:, pl.ds(0, count)], out_ref.at[pl.ds(width, spare), pl.ds(NEW_PAD, count)], sems.at[2]
            ),
            pltpu.make_async_copy(hidden, tail_ref, sems.at[3]),
        ]
        copies[0].start()
        copies[1].start()
        length = info_ref[1 + strags + mine]
        hidden[...] = jnp.where(iota2(hidden.shape, 1) < length, 0.0, HIDDEN).astype(BF16)
        copies[2].start()
        copies[3].start()
        for copy in copies:
            copy.wait()


def attend_kernel(strags, info_ref, query_ref, head_ref, tail_ref, keys_ref, out_ref, keys, raw_even, raw_odd, acc, total, top_even, top_odd, key_sems, tail_sem):
    mine = straggler_here(strags, info_ref)
    width, ctx = keys_ref.shape
    count = ctx // CHUNK
    factor = math.log2(math.e) / math.sqrt(NOPE + ROPE)

    def key_copy(i):
        part = pl.ds(pl.multiple_of(i * CHUNK, CHUNK), CHUNK)
        return pltpu.make_async_copy(keys_ref.at[:, part], keys.at[pl.ds(0, width), part], key_sems.at[i])

    def score(keys_part, raw, top):
        part = jnp.dot(query_ref[...], keys_part, preferred_element_type=F32)
        size = part.shape[1]
        raw[:, :size] = part
        peak = part[:, :128]
        for j in range(128, size, 128):
            peak = jnp.maximum(peak, part[:, j : j + 128])
        peak = jnp.broadcast_to(jnp.max(peak, axis=1, keepdims=True), peak.shape)
        return peak if top is None else jnp.maximum(top, peak)

    def weights(raw, size, shift):
        return [jnp.exp2(raw[:, j : j + 128] * factor - shift) for j in range(0, size, 128)]

    def gather(pieces, values_part, fade):
        mass = pieces[0]
        for piece in pieces[1:]:
            mass = mass + piece
        weight = pieces[0] if len(pieces) == 1 else jnp.concatenate(pieces, axis=1)
        value = lax.dot_general(weight.astype(BF16), values_part, (((1,), (1,)), ((), ())), preferred_element_type=F32)
        if fade is None:
            total[...] = mass
            acc[...] = value
            return
        total[...] = total[...] * fade + mass
        for j in range(0, KVL, 128):
            acc[:, j : j + 128] = acc[:, j : j + 128] * fade + value[:, j : j + 128]

    def step(keys_next, raw_next, top_next, values_now, raw_now, top_now, size_now, start):
        top = top_now[...]
        shift = top * factor
        fade = None if start else jnp.exp2(top_next[...] * factor - shift)
        pieces = weights(raw_now, size_now, shift)
        if keys_next is not None:
            top_next[...] = score(keys_next, raw_next, top)
        gather(pieces, values_now, fade)

    @pl.when(mine >= 0)
    def _():
        masks = pltpu.make_async_copy(tail_ref, keys.at[pl.ds(width, WIDE - width)], tail_sem)
        masks.start()
        for i in range(count):
            key_copy(i).start()

        def cached(i, depth):
            return keys[:depth, pl.ds(pl.multiple_of(i * CHUNK, CHUNK), CHUNK)]

        top_odd[...] = score(head_ref[:, :NEW_PAD], raw_odd, None)
        step(head_ref[:, NEW_PAD:], raw_even, top_even, head_ref[:KVL, :NEW_PAD], raw_odd, top_odd, NEW_PAD, True)
        masks.wait()
        key_copy(0).wait()

        @pl.loop(0, count // 2)
        def _(pair):
            i = pair * 2
            key_copy(i + 1).wait()
            key_copy(i + 2).wait()
            step(cached(i + 1, WIDE), raw_odd, top_odd, cached(i, KVL), raw_even, top_even, CHUNK, False)
            step(cached(i + 2, WIDE), raw_even, top_even, cached(i + 1, KVL), raw_odd, top_odd, CHUNK, False)

        step(None, None, top_odd, cached(count - 1, KVL), raw_even, top_even, CHUNK, False)
        inverse = 1.0 / jnp.sum(total[...], axis=1, keepdims=True)
        out_ref[...] = (acc[...] * inverse).astype(BF16)


def collect_kernel(strags, toks, heads, owners_ref, got_ref, out_ref, held):
    per = toks * heads
    for s in range(strags):
        held[s * per : (s + 1) * per, :] = got_ref[owners_ref[s]]
    shape = (toks * strags, strags * per)
    row, col = iota2(shape, 0), iota2(shape, 1)
    for h in range(heads):
        pick = (col == row % strags * per + row // strags * heads + h).astype(F32).astype(BF16)
        lined = jnp.dot(pick, held[...], preferred_element_type=F32).astype(BF16)
        for t in range(toks):
            out_ref[t, :, h * KVL : (h + 1) * KVL] = lined[t * strags : (t + 1) * strags]


def shards(cache, lengths, owners, positions, q_nope, q_rope, absorb_weight, new_latent):
    ranks = lax.axis_size("seq")
    me = lax.axis_index("seq").astype(jnp.int32).reshape(1)
    strags, toks = positions.shape
    heads = absorb_weight.shape[0]
    per = toks * heads
    ctx, width = cache.shape[1:]
    rows = ranks * per
    smem = pl.BlockSpec(memory_space=pltpu.SMEM)
    vmem = pl.BlockSpec(memory_space=pltpu.VMEM)
    anyspace = pl.BlockSpec(memory_space=pl.ANY)
    sending = pl.pallas_call(
        functools.partial(absorb_kernel, strags, toks, heads),
        out_shape=jax.ShapeDtypeStruct((ranks, per, WIDE), BF16),
        in_specs=[smem, anyspace, anyspace, anyspace],
        out_specs=anyspace,
        scratch_shapes=[
            VMEM((toks, strags, heads * NOPE), BF16),
            VMEM((toks, strags, heads * ROPE), BF16),
            VMEM((heads * NOPE, KVL), BF16),
            VMEM((toks * strags, heads * NOPE), F32),
            VMEM((toks * strags, heads * ROPE), F32),
            VMEM((strags * per, WIDE), BF16),
            pltpu.SemaphoreType.DMA((3,)),
            pltpu.SemaphoreType.DMA((strags,)),
        ],
        compiler_params=pltpu.CompilerParams(vmem_limit_bytes=60 * 2**20),
        name="absorb",
    )(
        owners,
        jnp.transpose(q_nope, (1, 0, 2)),
        jnp.transpose(q_rope, (1, 0, 2)),
        absorb_weight.reshape(heads * NOPE, KVL),
    )
    query = lax.all_to_all(sending, "seq", split_axis=0, concat_axis=0, tiled=True).reshape(rows, WIDE)
    seen = positions[:, None, :] <= positions[:, :, None]
    hidden = jnp.where(seen, 0.0, HIDDEN).astype(BF16)
    fresh = jnp.concatenate([jnp.transpose(new_latent, (0, 2, 1)), hidden], axis=1)
    fresh = jnp.pad(fresh, ((0, 0), (0, WIDE - width - toks), (0, 0)))
    unused = jnp.where(jnp.arange(WIDE) < width, 0.0, HIDDEN).astype(BF16)
    unused = jnp.broadcast_to(unused[None, :, None], (strags, WIDE, NEW_PAD - toks))
    fresh = jnp.concatenate([fresh, unused], axis=2)
    keys = jnp.transpose(cache[0])
    info = jnp.concatenate([me, owners, lengths])
    staged, masks = pl.pallas_call(
        functools.partial(stage_kernel, strags),
        out_shape=[jax.ShapeDtypeStruct((WIDE, HEAD), BF16), jax.ShapeDtypeStruct((WIDE - width, ctx), BF16)],
        in_specs=[smem, anyspace, anyspace],
        out_specs=[anyspace, anyspace],
        scratch_shapes=[VMEM((WIDE - width, ctx), BF16), pltpu.SemaphoreType.DMA((4,))],
        compiler_params=pltpu.CompilerParams(vmem_limit_bytes=24 * 2**20),
        cost_estimate=pl.CostEstimate(flops=0, bytes_accessed=4 * WIDE * HEAD, transcendentals=0),
        name="stage",
    )(info, fresh, keys)
    answer = pl.pallas_call(
        functools.partial(attend_kernel, strags),
        out_shape=jax.ShapeDtypeStruct((rows, KVL), BF16),
        in_specs=[smem, vmem, vmem, anyspace, anyspace],
        out_specs=vmem,
        scratch_shapes=[
            VMEM((WIDE, ctx), BF16),
            VMEM((rows, CHUNK), F32),
            VMEM((rows, CHUNK), F32),
            VMEM((rows, KVL), F32),
            VMEM((rows, 128), F32),
            VMEM((rows, 128), F32),
            VMEM((rows, 128), F32),
            pltpu.SemaphoreType.DMA((ctx // CHUNK,)),
            pltpu.SemaphoreType.DMA,
        ],
        compiler_params=pltpu.CompilerParams(vmem_limit_bytes=48 * 2**20),
        name="attend",
    )(info, query, staged, masks, keys)
    got = lax.all_to_all(answer.reshape(ranks, per, KVL), "seq", split_axis=0, concat_axis=0, tiled=True)
    out = pl.pallas_call(
        functools.partial(collect_kernel, strags, toks, heads),
        out_shape=jax.ShapeDtypeStruct((toks, strags, heads * KVL), BF16),
        in_specs=[smem, vmem],
        out_specs=vmem,
        scratch_shapes=[VMEM((strags * per, KVL), BF16)],
        compiler_params=pltpu.CompilerParams(vmem_limit_bytes=32 * 2**20),
        name="collect",
    )(owners, got)
    return jnp.transpose(out, (1, 0, 2))


def solution(mesh):
    in_specs = (
        P(("grp", "seq"), None, None),
        P("grp"),
        P("grp"),
        P("grp", None),
        P("grp", None, "seq"),
        P("grp", None, "seq"),
        P("seq", None, None),
        P("grp", None, None),
    )
    out_specs = P("grp", None, "seq")
    return jax.shard_map(shards, mesh=mesh, in_specs=in_specs, out_specs=out_specs, check_vma=False)
```

```python
import functools
import math

import jax
import jax.numpy as jnp
from jax import lax
from jax.experimental import pallas as pl
from jax.experimental.pallas import tpu as pltpu
from jax.sharding import PartitionSpec as P

KVL = 512
ROPE = 64
NOPE = 128
NEW_PAD = 128
CHUNK = 1024
HEAD = NEW_PAD + CHUNK
F32 = jnp.float32
BF16 = jnp.bfloat16
HIDDEN = -1e30
WIDE = 640
VMEM = pltpu.VMEM


def iota2(shape, dim):
    return lax.broadcasted_iota(jnp.int32, shape, dim)


def absorb_kernel(strags, toks, heads, owners_ref, nope_hbm, rope_hbm, weight_hbm, out_hbm, nope_ref, rope_ref, weight_ref, nope_rows, rope_rows, slots, sems, out_sems):
    copies = [
        pltpu.make_async_copy(src, dst, sems.at[i])
        for i, (src, dst) in enumerate(((nope_hbm, nope_ref), (rope_hbm, rope_ref), (weight_hbm, weight_ref)))
    ]
    for copy in copies:
        copy.start()
    per = toks * heads
    rows = strags * per

    def parts_of(shape):
        row = iota2(shape, 0)
        strag = sum((row >= s * per).astype(jnp.int32) for s in range(1, strags))
        line = row - strag * per
        return strag, line // heads, line & (heads - 1)

    shape = (rows, toks * strags)
    strag, tok, _ = parts_of(shape)
    pick = (iota2(shape, 1) == tok * strags + strag).astype(F32).astype(BF16)
    shape = (heads * ROPE, ROPE)
    fold = ((iota2(shape, 0) & (ROPE - 1)) == iota2(shape, 1)).astype(F32).astype(BF16)
    shape = (rows, WIDE - KVL - ROPE)
    marks = (iota2(shape, 1) == parts_of(shape)[1]).astype(F32).astype(BF16)
    _, _, head = parts_of((rows, 1))

    def spread(ref, width):
        copied = jnp.dot(pick, ref[...].astype(BF16), preferred_element_type=F32)
        pieces = []
        for h in range(heads):
            pieces.append(jnp.where(head == h, copied[:, h * width : (h + 1) * width], 0.0))
        return pieces

    copies[0].wait()
    copies[1].wait()
    for t in range(toks):
        nope_rows[t * strags : (t + 1) * strags, :] = nope_ref[t].astype(F32)
        rope_rows[t * strags : (t + 1) * strags, :] = rope_ref[t].astype(F32)
    expanded = jnp.concatenate(spread(nope_rows, NOPE), axis=1).astype(BF16)
    roped = sum(spread(rope_rows, ROPE)).astype(BF16)
    slots[:, KVL:] = jnp.concatenate([roped, marks], axis=1)
    copies[2].wait()
    slots[:, :KVL] = jnp.dot(expanded, weight_ref[...], preferred_element_type=F32).astype(BF16)
    leaving = [
        pltpu.make_async_copy(slots.at[pl.ds(s * per, per)], out_hbm.at[owners_ref[s]], out_sems.at[s]) for s in range(strags)
    ]
    for copy in leaving:
        copy.start()
    for copy in leaving:
        copy.wait()


def straggler_here(strags, info_ref):
    mine = jnp.int32(-1)
    for s in range(strags):
        mine = jnp.where(info_ref[1 + s] == info_ref[0], s, mine)
    return mine


def stage_kernel(strags, info_ref, new_ref, keys_ref, out_ref, hidden, sems):
    mine = straggler_here(strags, info_ref)
    width = keys_ref.shape[0]
    count = out_ref.shape[1] - NEW_PAD

    @pl.when(mine >= 0)
    def _():
        copies = [
            pltpu.make_async_copy(
                keys_ref.at[:, pl.ds(0, count)], out_ref.at[pl.ds(0, width), pl.ds(NEW_PAD, count)], sems.at[0]
            ),
            pltpu.make_async_copy(new_ref.at[mine], out_ref.at[:, pl.ds(0, NEW_PAD)], sems.at[1]),
            pltpu.make_async_copy(hidden, out_ref.at[pl.ds(width, WIDE - width), pl.ds(NEW_PAD, count)], sems.at[2]),
        ]
        copies[0].start()
        copies[1].start()
        length = info_ref[1 + strags + mine]
        hidden[...] = jnp.where(iota2(hidden.shape, 1) < length, 0.0, HIDDEN).astype(BF16)
        copies[2].start()
        for copy in copies:
            copy.wait()


def attend_kernel(strags, info_ref, query_ref, head_ref, keys_ref, out_ref, keys, raw_even, raw_odd, acc, total, top_even, top_odd, key_sems):
    mine = straggler_here(strags, info_ref)
    width, ctx = keys_ref.shape
    first = head_ref.shape[1] - NEW_PAD
    late = [(at, min(CHUNK, ctx - first - at)) for at in range(0, ctx - first, CHUNK)]
    factor = math.log2(math.e) / math.sqrt(NOPE + ROPE)

    def key_copy(i):
        at, size = late[i]
        source, target = pl.ds(first + at, size), pl.ds(at, size)
        return pltpu.make_async_copy(keys_ref.at[:, source], keys.at[pl.ds(0, width), target], key_sems.at[i])

    def score(keys_part, raw, top):
        part = jnp.dot(query_ref[...], keys_part, preferred_element_type=F32)
        size = part.shape[1]
        raw[:, :size] = part
        peak = part[:, :128]
        for j in range(128, size, 128):
            peak = jnp.maximum(peak, part[:, j : j + 128])
        peak = jnp.broadcast_to(jnp.max(peak, axis=1, keepdims=True), peak.shape)
        return peak if top is None else jnp.maximum(top, peak)

    def weights(raw, size, shift):
        return [jnp.exp2(raw[:, j : j + 128] * factor - shift) for j in range(0, size, 128)]

    def gather(pieces, values_part, fade):
        mass = pieces[0]
        for piece in pieces[1:]:
            mass = mass + piece
        weight = pieces[0] if len(pieces) == 1 else jnp.concatenate(pieces, axis=1)
        value = lax.dot_general(weight.astype(BF16), values_part, (((1,), (1,)), ((), ())), preferred_element_type=F32)
        if fade is None:
            total[...] = mass
            acc[...] = value
            return
        total[...] = total[...] * fade + mass
        for j in range(0, KVL, 128):
            acc[:, j : j + 128] = acc[:, j : j + 128] * fade + value[:, j : j + 128]

    def step(keys_next, raw_next, top_next, values_now, raw_now, top_now, size_now, start):
        top = top_now[...]
        before = None if start else top_next[...]
        if keys_next is not None:
            top_next[...] = score(keys_next, raw_next, top)
        shift = top * factor
        fade = None if start else jnp.exp2(before * factor - shift)
        pieces = weights(raw_now, size_now, shift)
        gather(pieces, values_now, fade)

    @pl.when(mine >= 0)
    def _():
        for i in range(len(late)):
            key_copy(i).start()
        length = info_ref[1 + strags + mine]
        spare = (WIDE - width, ctx - first)
        keys[width:, :] = jnp.where(first + iota2(spare, 1) < length, 0.0, HIDDEN).astype(BF16)

        now, after = (raw_odd, top_odd), (raw_even, top_even)
        now[1][...] = score(head_ref[:, :NEW_PAD], now[0], None)
        step(head_ref[:, NEW_PAD:], *after, head_ref[:KVL, :NEW_PAD], *now, NEW_PAD, True)
        values, held = head_ref[:KVL, NEW_PAD:], first
        for i, (at, size) in enumerate(late):
            now, after = after, now
            key_copy(i).wait()
            step(keys[:, at : at + size], *after, values, *now, held, False)
            values, held = keys[:KVL, at : at + size], size
        now, after = after, now
        step(None, None, after[1], values, *now, held, False)
        inverse = 1.0 / jnp.sum(total[...], axis=1, keepdims=True)
        out_ref[...] = (acc[...] * inverse).astype(BF16)


def collect_kernel(strags, toks, heads, owners_ref, got_ref, out_ref, held):
    per = toks * heads
    for s in range(strags):
        held[s * per : (s + 1) * per, :] = got_ref[owners_ref[s]]
    shape = (toks * strags, strags * per)
    row, col = iota2(shape, 0), iota2(shape, 1)
    for h in range(heads):
        pick = (col == row % strags * per + row // strags * heads + h).astype(F32).astype(BF16)
        lined = jnp.dot(pick, held[...], preferred_element_type=F32).astype(BF16)
        for t in range(toks):
            out_ref[t, :, h * KVL : (h + 1) * KVL] = lined[t * strags : (t + 1) * strags]


def shards(cache, lengths, owners, positions, q_nope, q_rope, absorb_weight, new_latent):
    ranks = lax.axis_size("seq")
    me = lax.axis_index("seq").astype(jnp.int32).reshape(1)
    strags, toks = positions.shape
    heads = absorb_weight.shape[0]
    per = toks * heads
    ctx, width = cache.shape[1:]
    rows = ranks * per
    smem = pl.BlockSpec(memory_space=pltpu.SMEM)
    vmem = pl.BlockSpec(memory_space=pltpu.VMEM)
    anyspace = pl.BlockSpec(memory_space=pl.ANY)
    sending = pl.pallas_call(
        functools.partial(absorb_kernel, strags, toks, heads),
        out_shape=jax.ShapeDtypeStruct((ranks, per, WIDE), BF16),
        in_specs=[smem, anyspace, anyspace, anyspace],
        out_specs=anyspace,
        scratch_shapes=[
            VMEM((toks, strags, heads * NOPE), BF16),
            VMEM((toks, strags, heads * ROPE), BF16),
            VMEM((heads * NOPE, KVL), BF16),
            VMEM((toks * strags, heads * NOPE), F32),
            VMEM((toks * strags, heads * ROPE), F32),
            VMEM((strags * per, WIDE), BF16),
            pltpu.SemaphoreType.DMA((3,)),
            pltpu.SemaphoreType.DMA((strags,)),
        ],
        compiler_params=pltpu.CompilerParams(vmem_limit_bytes=60 * 2**20),
        name="absorb",
    )(
        owners,
        jnp.transpose(q_nope, (1, 0, 2)),
        jnp.transpose(q_rope, (1, 0, 2)),
        absorb_weight.reshape(heads * NOPE, KVL),
    )
    query = lax.all_to_all(sending, "seq", split_axis=0, concat_axis=0, tiled=True).reshape(rows, WIDE)
    seen = positions[:, None, :] <= positions[:, :, None]
    hidden = jnp.where(seen, 0.0, HIDDEN).astype(BF16)
    fresh = jnp.concatenate([jnp.transpose(new_latent, (0, 2, 1)), hidden], axis=1)
    fresh = jnp.pad(fresh, ((0, 0), (0, WIDE - width - toks), (0, 0)))
    unused = jnp.where(jnp.arange(WIDE) < width, 0.0, HIDDEN).astype(BF16)
    unused = jnp.broadcast_to(unused[None, :, None], (strags, WIDE, NEW_PAD - toks))
    fresh = jnp.concatenate([fresh, unused], axis=2)
    keys = jnp.transpose(cache[0])
    info = jnp.concatenate([me, owners, lengths])
    staged = pl.pallas_call(
        functools.partial(stage_kernel, strags),
        out_shape=jax.ShapeDtypeStruct((WIDE, HEAD), BF16),
        in_specs=[smem, anyspace, anyspace],
        out_specs=anyspace,
        scratch_shapes=[VMEM((WIDE - width, HEAD - NEW_PAD), BF16), pltpu.SemaphoreType.DMA((3,))],
        compiler_params=pltpu.CompilerParams(vmem_limit_bytes=24 * 2**20),
        cost_estimate=pl.CostEstimate(flops=0, bytes_accessed=4 * WIDE * HEAD, transcendentals=0),
        name="stage",
    )(info, fresh, keys)
    late = ctx - (HEAD - NEW_PAD)
    answer = pl.pallas_call(
        functools.partial(attend_kernel, strags),
        out_shape=jax.ShapeDtypeStruct((rows, KVL), BF16),
        in_specs=[smem, vmem, vmem, anyspace],
        out_specs=vmem,
        scratch_shapes=[
            VMEM((WIDE, late), BF16),
            VMEM((rows, CHUNK), F32),
            VMEM((rows, CHUNK), F32),
            VMEM((rows, KVL), F32),
            VMEM((rows, 128), F32),
            VMEM((rows, 128), F32),
            VMEM((rows, 128), F32),
            pltpu.SemaphoreType.DMA((pl.cdiv(late, CHUNK),)),
        ],
        compiler_params=pltpu.CompilerParams(vmem_limit_bytes=48 * 2**20),
        name="attend",
    )(info, query, staged, keys)
    got = lax.all_to_all(answer.reshape(ranks, per, KVL), "seq", split_axis=0, concat_axis=0, tiled=True)
    out = pl.pallas_call(
        functools.partial(collect_kernel, strags, toks, heads),
        out_shape=jax.ShapeDtypeStruct((toks, strags, heads * KVL), BF16),
        in_specs=[smem, vmem],
        out_specs=vmem,
        scratch_shapes=[VMEM((strags * per, KVL), BF16)],
        compiler_params=pltpu.CompilerParams(vmem_limit_bytes=32 * 2**20),
        name="collect",
    )(owners, got)
    return jnp.transpose(out, (1, 0, 2))


def solution(mesh):
    in_specs = (
        P(("grp", "seq"), None, None),
        P("grp"),
        P("grp"),
        P("grp", None),
        P("grp", None, "seq"),
        P("grp", None, "seq"),
        P("seq", None, None),
        P("grp", None, None),
    )
    out_specs = P("grp", None, "seq")
    return jax.shard_map(shards, mesh=mesh, in_specs=in_specs, out_specs=out_specs, check_vma=False)
```

```python
import functools
import math

import jax
import jax.numpy as jnp
from jax import lax
from jax.experimental import pallas as pl
from jax.experimental.pallas import tpu as pltpu
from jax.sharding import PartitionSpec as P

KVL = 512
ROPE = 64
NOPE = 128
NEW_PAD = 128
CHUNK = 512
HEAD = NEW_PAD + 2 * CHUNK
F32 = jnp.float32
BF16 = jnp.bfloat16
HIDDEN = -1e30
WIDE = 640
VMEM = pltpu.VMEM


def iota2(shape, dim):
    return lax.broadcasted_iota(jnp.int32, shape, dim)


def absorb_kernel(strags, toks, heads, owners_ref, nope_hbm, rope_hbm, weight_hbm, out_hbm, nope_ref, rope_ref, weight_ref, nope_rows, rope_rows, slots, sems, out_sems):
    copies = [
        pltpu.make_async_copy(src, dst, sems.at[i])
        for i, (src, dst) in enumerate(((nope_hbm, nope_ref), (rope_hbm, rope_ref), (weight_hbm, weight_ref)))
    ]
    for copy in copies:
        copy.start()
    per = toks * heads
    rows = strags * per

    def parts_of(shape):
        row = iota2(shape, 0)
        strag = sum((row >= s * per).astype(jnp.int32) for s in range(1, strags))
        line = row - strag * per
        return strag, line // heads, line & (heads - 1)

    shape = (rows, toks * strags)
    strag, tok, _ = parts_of(shape)
    pick = (iota2(shape, 1) == tok * strags + strag).astype(F32).astype(BF16)
    shape = (heads * ROPE, ROPE)
    fold = ((iota2(shape, 0) & (ROPE - 1)) == iota2(shape, 1)).astype(F32).astype(BF16)
    shape = (rows, WIDE - KVL - ROPE)
    marks = (iota2(shape, 1) == parts_of(shape)[1]).astype(F32).astype(BF16)
    _, _, head = parts_of((rows, 1))

    def spread(ref, width):
        copied = jnp.dot(pick, ref[...].astype(BF16), preferred_element_type=F32)
        pieces = []
        for h in range(heads):
            pieces.append(jnp.where(head == h, copied[:, h * width : (h + 1) * width], 0.0))
        return pieces

    copies[0].wait()
    copies[1].wait()
    for t in range(toks):
        nope_rows[t * strags : (t + 1) * strags, :] = nope_ref[t].astype(F32)
        rope_rows[t * strags : (t + 1) * strags, :] = rope_ref[t].astype(F32)
    expanded = jnp.concatenate(spread(nope_rows, NOPE), axis=1).astype(BF16)
    roped = sum(spread(rope_rows, ROPE)).astype(BF16)
    slots[:, KVL:] = jnp.concatenate([roped, marks], axis=1)
    copies[2].wait()
    slots[:, :KVL] = jnp.dot(expanded, weight_ref[...], preferred_element_type=F32).astype(BF16)
    leaving = [
        pltpu.make_async_copy(slots.at[pl.ds(s * per, per)], out_hbm.at[owners_ref[s]], out_sems.at[s]) for s in range(strags)
    ]
    for copy in leaving:
        copy.start()
    for copy in leaving:
        copy.wait()


def straggler_here(strags, info_ref):
    mine = jnp.int32(-1)
    for s in range(strags):
        mine = jnp.where(info_ref[1 + s] == info_ref[0], s, mine)
    return mine


def stage_kernel(strags, info_ref, new_ref, keys_ref, out_ref, hidden, sems):
    mine = straggler_here(strags, info_ref)
    width = keys_ref.shape[0]
    count = out_ref.shape[1] - NEW_PAD

    @pl.when(mine >= 0)
    def _():
        copies = [
            pltpu.make_async_copy(
                keys_ref.at[:, pl.ds(0, count)], out_ref.at[pl.ds(0, width), pl.ds(NEW_PAD, count)], sems.at[0]
            ),
            pltpu.make_async_copy(new_ref.at[mine], out_ref.at[:, pl.ds(0, NEW_PAD)], sems.at[1]),
            pltpu.make_async_copy(hidden, out_ref.at[pl.ds(width, WIDE - width), pl.ds(NEW_PAD, count)], sems.at[2]),
        ]
        copies[0].start()
        copies[1].start()
        length = info_ref[1 + strags + mine]
        hidden[...] = jnp.where(iota2(hidden.shape, 1) < length, 0.0, HIDDEN).astype(BF16)
        copies[2].start()
        for copy in copies:
            copy.wait()


def attend_kernel(strags, info_ref, query_ref, head_ref, keys_ref, out_ref, keys, raw_even, raw_odd, acc, total, top_even, top_odd, key_sems):
    mine = straggler_here(strags, info_ref)
    width, ctx = keys_ref.shape
    first = head_ref.shape[1] - NEW_PAD
    count = (ctx - first) // CHUNK
    factor = math.log2(math.e) / math.sqrt(NOPE + ROPE)

    def key_copy(i):
        source = pl.ds(pl.multiple_of(first + i * CHUNK, CHUNK), CHUNK)
        target = pl.ds(pl.multiple_of(i * CHUNK, CHUNK), CHUNK)
        return pltpu.make_async_copy(keys_ref.at[:, source], keys.at[pl.ds(0, width), target], key_sems.at[i])

    def score(keys_part, raw, top):
        part = jnp.dot(query_ref[...], keys_part, preferred_element_type=F32)
        size = part.shape[1]
        raw[:, :size] = part
        peak = part[:, :128]
        for j in range(128, size, 128):
            peak = jnp.maximum(peak, part[:, j : j + 128])
        peak = jnp.broadcast_to(jnp.max(peak, axis=1, keepdims=True), peak.shape)
        return peak if top is None else jnp.maximum(top, peak)

    def weights(raw, size, shift):
        return [jnp.exp2(raw[:, j : j + 128] * factor - shift) for j in range(0, size, 128)]

    def gather(pieces, values_part, fade):
        mass = pieces[0]
        for piece in pieces[1:]:
            mass = mass + piece
        weight = pieces[0] if len(pieces) == 1 else jnp.concatenate(pieces, axis=1)
        value = lax.dot_general(weight.astype(BF16), values_part, (((1,), (1,)), ((), ())), preferred_element_type=F32)
        if fade is None:
            total[...] = mass
            acc[...] = value
            return
        total[...] = total[...] * fade + mass
        for j in range(0, KVL, 128):
            acc[:, j : j + 128] = acc[:, j : j + 128] * fade + value[:, j : j + 128]

    def step(keys_next, raw_next, top_next, values_now, raw_now, top_now, size_now, start):
        top = top_now[...]
        before = None if start else top_next[...]
        if keys_next is not None:
            top_next[...] = score(keys_next, raw_next, top)
        shift = top * factor
        fade = None if start else jnp.exp2(before * factor - shift)
        pieces = weights(raw_now, size_now, shift)
        gather(pieces, values_now, fade)

    @pl.when(mine >= 0)
    def _():
        for i in range(count):
            key_copy(i).start()
        length = info_ref[1 + strags + mine]
        spare = (WIDE - width, ctx - first)
        keys[width:, :] = jnp.where(first + iota2(spare, 1) < length, 0.0, HIDDEN).astype(BF16)

        def cached(i, depth):
            return keys[:depth, pl.ds(pl.multiple_of(i * CHUNK, CHUNK), CHUNK)]

        second = NEW_PAD + CHUNK
        top_odd[...] = score(head_ref[:, :NEW_PAD], raw_odd, None)
        step(head_ref[:, NEW_PAD:second], raw_even, top_even, head_ref[:KVL, :NEW_PAD], raw_odd, top_odd, NEW_PAD, True)
        step(head_ref[:, second:], raw_odd, top_odd, head_ref[:KVL, NEW_PAD:second], raw_even, top_even, CHUNK, False)
        key_copy(0).wait()
        step(cached(0, WIDE), raw_even, top_even, head_ref[:KVL, second:], raw_odd, top_odd, CHUNK, False)

        @pl.loop(0, count // 2)
        def _(pair):
            i = pair * 2
            key_copy(i + 1).wait()
            step(cached(i + 1, WIDE), raw_odd, top_odd, cached(i, KVL), raw_even, top_even, CHUNK, False)
            key_copy(i + 2).wait()
            step(cached(i + 2, WIDE), raw_even, top_even, cached(i + 1, KVL), raw_odd, top_odd, CHUNK, False)

        step(None, None, top_odd, cached(count - 1, KVL), raw_even, top_even, CHUNK, False)
        inverse = 1.0 / jnp.sum(total[...], axis=1, keepdims=True)
        out_ref[...] = (acc[...] * inverse).astype(BF16)


def collect_kernel(strags, toks, heads, owners_ref, got_ref, out_ref):
    per = toks * heads
    held = jnp.concatenate([got_ref[owners_ref[s]] for s in range(strags)], axis=0)
    shape = (toks * strags, strags * per)
    row, col = iota2(shape, 0), iota2(shape, 1)
    for h in range(heads):
        pick = (col == row % strags * per + row // strags * heads + h).astype(F32).astype(BF16)
        lined = jnp.dot(pick, held, preferred_element_type=F32).astype(BF16)
        for t in range(toks):
            out_ref[t, :, h * KVL : (h + 1) * KVL] = lined[t * strags : (t + 1) * strags]


def shards(cache, lengths, owners, positions, q_nope, q_rope, absorb_weight, new_latent):
    ranks = lax.axis_size("seq")
    me = lax.axis_index("seq").astype(jnp.int32).reshape(1)
    strags, toks = positions.shape
    heads = absorb_weight.shape[0]
    per = toks * heads
    ctx, width = cache.shape[1:]
    rows = ranks * per
    smem = pl.BlockSpec(memory_space=pltpu.SMEM)
    vmem = pl.BlockSpec(memory_space=pltpu.VMEM)
    anyspace = pl.BlockSpec(memory_space=pl.ANY)
    sending = pl.pallas_call(
        functools.partial(absorb_kernel, strags, toks, heads),
        out_shape=jax.ShapeDtypeStruct((ranks, per, WIDE), BF16),
        in_specs=[smem, anyspace, anyspace, anyspace],
        out_specs=anyspace,
        scratch_shapes=[
            VMEM((toks, strags, heads * NOPE), BF16),
            VMEM((toks, strags, heads * ROPE), BF16),
            VMEM((heads * NOPE, KVL), BF16),
            VMEM((toks * strags, heads * NOPE), F32),
            VMEM((toks * strags, heads * ROPE), F32),
            VMEM((strags * per, WIDE), BF16),
            pltpu.SemaphoreType.DMA((3,)),
            pltpu.SemaphoreType.DMA((strags,)),
        ],
        compiler_params=pltpu.CompilerParams(vmem_limit_bytes=60 * 2**20),
        name="absorb",
    )(
        owners,
        jnp.transpose(q_nope, (1, 0, 2)),
        jnp.transpose(q_rope, (1, 0, 2)),
        absorb_weight.reshape(heads * NOPE, KVL),
    )
    query = lax.all_to_all(sending, "seq", split_axis=0, concat_axis=0, tiled=True).reshape(rows, WIDE)
    seen = positions[:, None, :] <= positions[:, :, None]
    hidden = jnp.where(seen, 0.0, HIDDEN).astype(BF16)
    fresh = jnp.concatenate([jnp.transpose(new_latent, (0, 2, 1)), hidden], axis=1)
    fresh = jnp.pad(fresh, ((0, 0), (0, WIDE - width - toks), (0, 0)))
    unused = jnp.where(jnp.arange(WIDE) < width, 0.0, HIDDEN).astype(BF16)
    unused = jnp.broadcast_to(unused[None, :, None], (strags, WIDE, NEW_PAD - toks))
    fresh = jnp.concatenate([fresh, unused], axis=2)
    keys = jnp.transpose(cache[0])
    info = jnp.concatenate([me, owners, lengths])
    staged = pl.pallas_call(
        functools.partial(stage_kernel, strags),
        out_shape=jax.ShapeDtypeStruct((WIDE, HEAD), BF16),
        in_specs=[smem, anyspace, anyspace],
        out_specs=anyspace,
        scratch_shapes=[VMEM((WIDE - width, HEAD - NEW_PAD), BF16), pltpu.SemaphoreType.DMA((3,))],
        compiler_params=pltpu.CompilerParams(vmem_limit_bytes=24 * 2**20),
        cost_estimate=pl.CostEstimate(flops=0, bytes_accessed=4 * WIDE * HEAD, transcendentals=0),
        name="stage",
    )(info, fresh, keys)
    late = ctx - (HEAD - NEW_PAD)
    answer = pl.pallas_call(
        functools.partial(attend_kernel, strags),
        out_shape=jax.ShapeDtypeStruct((rows, KVL), BF16),
        in_specs=[smem, vmem, vmem, anyspace],
        out_specs=vmem,
        scratch_shapes=[
            VMEM((WIDE, late), BF16),
            VMEM((rows, CHUNK), F32),
            VMEM((rows, CHUNK), F32),
            VMEM((rows, KVL), F32),
            VMEM((rows, 128), F32),
            VMEM((rows, 128), F32),
            VMEM((rows, 128), F32),
            pltpu.SemaphoreType.DMA((late // CHUNK,)),
        ],
        compiler_params=pltpu.CompilerParams(vmem_limit_bytes=48 * 2**20),
        name="attend",
    )(info, query, staged, keys)
    got = lax.all_to_all(answer.reshape(ranks, per, KVL), "seq", split_axis=0, concat_axis=0, tiled=True)
    out = pl.pallas_call(
        functools.partial(collect_kernel, strags, toks, heads),
        out_shape=jax.ShapeDtypeStruct((toks, strags, heads * KVL), BF16),
        in_specs=[smem, vmem],
        out_specs=vmem,
        compiler_params=pltpu.CompilerParams(vmem_limit_bytes=32 * 2**20),
        name="collect",
    )(owners, got)
    return jnp.transpose(out, (1, 0, 2))


def solution(mesh):
    in_specs = (
        P(("grp", "seq"), None, None),
        P("grp"),
        P("grp"),
        P("grp", None),
        P("grp", None, "seq"),
        P("grp", None, "seq"),
        P("seq", None, None),
        P("grp", None, None),
    )
    out_specs = P("grp", None, "seq")
    return jax.shard_map(shards, mesh=mesh, in_specs=in_specs, out_specs=out_specs, check_vma=False)
```
